32 devices in a mesh: groups: 2 (over y), basis: 4 (over z), dp: 2 (over x), sub: 2 (over core).
Axes of the slice: x: 2, y: 2, z: 4, core: 2. Of those that a mesh axis runs over, the one named last changes fastest.
Arguments:
- activations: bfloat16 [4096, 8192], P(('groups', 'dp'), 'basis'), parts along dimension 0, may hold values from -6 to 6
- gradients: bfloat16 [4096, 28672], P(('groups', 'dp'), 'basis'), parts along dimension 0, may hold values from -6 to 6
- act_basis: float32 [16384, 512], P(('groups', 'basis'), 'sub'), parts along dimension 0, may hold values from -0.09375 to 0.09375
- grad_basis: float32 [57344, 1024], P(('groups', 'basis'), 'sub'), parts along dimension 0, may hold values from -0.046875 to 0.046875
Outputs:
- moments: float32 [2048, 512], P(('groups', 'sub', 'basis'), 'dp'), parts along dimension 0
The draws below stay inside these ranges and needn't reach their ends.
There are 2 independent parts, one for each index of `groups`. The reference program is written for one: setup_inputs(seed, part) draws one part's arguments, and reference() takes and returns one part's arrays. A program takes and returns all parts, laid end to end along the dimension named above; each array names one. Nothing has to cross between parts.
All inputs are finite; a program needn't handle non-finite values.
Results may differ from the reference program's by a relative error of at most 0.0003.
Values sent between devices are 32-bit elements; how exact they have to be, the bound alone decides.
A program may use at most 128 MiB of HBM per device.

```python
import jax
import jax.numpy as jnp
from jax import lax

D = 8192
F = 28672
KA = 512
KG = 1024
TOKENS = 2048


def strengthened(values, key, source, target, parts, factor):
    owner, partner = [(jnp.arange(values.shape[position]) // (values.shape[position] // parts)).reshape([-1 if axis == position else 1 for axis in range(values.ndim)]) for position in (source, target)]
    chosen = jax.random.permutation(key, parts)[partner]
    strong = (owner == chosen) | (owner == (partner + parts // 2) % parts)
    return jnp.where(strong, factor * values, values)


def steps_of(own_key, dims, split, least, top_value):
    gain = 1.0
    for position, parts in split:
        draws = jax.random.uniform(jax.random.fold_in(jax.random.fold_in(own_key, 6), position), (parts,), jnp.float32, least / len(split), top_value / len(split))
        gain = gain * jnp.repeat(jnp.exp(draws), dims[position] // parts).reshape((-1,) + (1,) * (len(dims) - 1 - position))
    return gain


def gaussian(rng, extent, width, most, cuts=(), dtype=jnp.bfloat16):
    entries = jax.random.normal(rng, extent, jnp.float32) * width
    if len(cuts) > 0:
        entries = steps_of(rng, extent, cuts, -0.22, 0.18) * entries
    return jnp.clip(entries, min=-most, max=most).astype(dtype)


def gaussian_with(stream_key, dims, spread, most, pieces, heavy, dtype=jnp.bfloat16):
    result = spread * jax.random.normal(stream_key, dims, jnp.float32)
    if pieces:
        result = result * steps_of(stream_key, dims, pieces, -0.22, 0.18)
    return jnp.clip(strengthened(result, jax.random.fold_in(stream_key, 3), *heavy), -most, most).astype(dtype)


def setup_inputs(seed: int = 0, part: int = 0) -> dict:
    key_list = jax.random.split(jax.random.key(seed), 5)
    own_keys = jax.random.split(jax.random.fold_in(key_list[4], part), 5)
    activations = gaussian(own_keys[0], (TOKENS, D), 1.0, 6.0, ((0, 2), (1, 4)))
    gradients = gaussian(own_keys[1], (TOKENS, F), 1.0, 6.0, ((0, 2), (1, 4)))
    act_basis = gaussian_with(own_keys[2], (D, KA), D ** -0.5, 0.09375, ((0, 4), (1, 2)), (0, 1, 4, 2.0), jnp.float32)
    grad_basis = gaussian_with(own_keys[3], (F, KG), F ** -0.5, 0.046875, ((0, 4), (1, 2)), (0, 1, 4, 2.0), jnp.float32)
    return dict(activations=activations, gradients=gradients, act_basis=act_basis, grad_basis=grad_basis)


def reference(activations, gradients, act_basis, grad_basis):
    proj_act = jnp.dot(activations.astype(jnp.float32), act_basis, precision=lax.Precision.HIGHEST)
    proj_grad = jnp.dot(gradients.astype(jnp.float32), grad_basis, precision=lax.Precision.HIGHEST)
    squared_act = proj_act * proj_act
    squared_grad = proj_grad * proj_grad
    total = lax.dot_general(squared_grad, squared_act, (((0,), (0,)), ((), ())), precision=lax.Precision.HIGHEST, preferred_element_type=jnp.float32)
    return total / TOKENS
```

```python
import jax
import jax.numpy as jnp
from jax import lax
from jax.sharding import PartitionSpec as P


def halves(basis):
    high = lax.reduce_precision(basis, 8, 7)
    return high.astype(jnp.bfloat16), (basis - high).astype(jnp.bfloat16)


def make_term(basis, rows_in):
    dims = (((0,), (1,)), ((), ()))
    high, low = halves(basis)
    return lax.dot_general(
        high, rows_in, dims, preferred_element_type=jnp.float32
    ) + lax.dot_general(low, rows_in, dims, preferred_element_type=jnp.float32)


def pair_products(left, right):
    return lax.dot_general(
        left,
        right,
        (((1,), (1,)), ((), ())),
        precision=lax.Precision.HIGHEST,
        preferred_element_type=jnp.float32,
    )


def body(activations, gradients, act_basis, grad_basis):
    full_act = lax.psum(make_term(act_basis, activations), "basis")
    own_grad = lax.psum_scatter(
        make_term(grad_basis, gradients), "basis", scatter_dimension=0, tiled=True
    )
    squared_act = lax.all_gather(full_act * full_act, "sub", axis=0, tiled=True)
    partial_sums = pair_products(own_grad * own_grad, squared_act)
    summed = lax.psum_scatter(partial_sums, "dp", scatter_dimension=1, tiled=True)
    return summed / (activations.shape[0] * lax.axis_size("dp"))


def solution(mesh):
    return jax.shard_map(
        body,
        mesh=mesh,
        in_specs=(
            P(("groups", "dp"), "basis"),
            P(("groups", "dp"), "basis"),
            P(("groups", "basis"), "sub"),
            P(("groups", "basis"), "sub"),
        ),
        out_specs=P(("groups", "sub", "basis"), "dp"),
        check_vma=False,
    )
```

```python
import functools

import jax
import jax.numpy as jnp
from jax import lax
from jax.experimental import pallas as pl
from jax.experimental.pallas import tpu as pltpu
from jax.sharding import PartitionSpec as P

MESH = pl.DeviceIdType.MESH
WAYS = 4
EVECS = 128
ROWS = 128
STEPS = 4


def chain_kernel(
    total_tokens,
    act_hbm,
    grad_hbm,
    act_basis_hbm,
    grad_basis_hbm,
    out_ref,
    act,
    grad,
    act_basis,
    grad_basis,
    split,
    acc,
    part,
    got,
    squares,
    x_out,
    x_in,
    sums,
    final,
    load_sem,
    send_sem,
    recv_sem,
    pair_sem,
    x_send,
    x_recv,
    final_send,
    final_recv,
):
    z = lax.axis_index("basis")
    d = lax.axis_index("dp")
    s = lax.axis_index("sub")
    tokens, features = act.shape
    half = tokens // 2
    act_blocks = act_basis.shape[1] // EVECS
    grad_blocks = grad_basis.shape[0]
    per_block = half // ROWS
    chunks = part.shape[1]
    act_chunks = act_blocks * per_block
    piece = grad.shape[1] // STEPS
    block_rows = (0, 3, 1, 2)

    barrier = pltpu.get_barrier_semaphore()
    for hop in range(1, WAYS):
        pl.semaphore_signal(
            barrier, inc=1, device_id={"basis": lax.rem(z + hop, WAYS)}, device_id_type=MESH
        )
    pl.semaphore_signal(barrier, inc=1, device_id={"dp": 1 - d}, device_id_type=MESH)
    pl.semaphore_signal(barrier, inc=1, device_id={"sub": 1 - s}, device_id_type=MESH)

    loads = [pltpu.make_async_copy(act_basis_hbm, act_basis, load_sem.at[0])]
    for way in range(2):
        rows = pl.ds(way * half, half)
        loads.append(
            pltpu.make_async_copy(act_hbm.at[rows, :], act.at[rows, :], load_sem.at[1 + way])
        )
    for way in range(2):
        rows = pl.ds(way * half, half)
        loads.append(
            pltpu.make_async_copy(grad_hbm.at[rows, :], grad.at[rows, :], load_sem.at[3 + way])
        )

    def load_block(i):
        column = block_rows[i] * EVECS
        return pltpu.make_async_copy(
            grad_basis_hbm.at[:, pl.ds(column, EVECS)], grad_basis.at[i], load_sem.at[5 + i]
        )

    for load in loads[:3]:
        load.start()
    load_block(0).start()
    for load in loads[3:]:
        load.start()
    pl.semaphore_wait(barrier, WAYS + 1)

    def hops(way):
        return z if way else WAYS - 1 - z

    def chunk_copy(way, c):
        to = lax.rem(z + (1 if way else WAYS - 1), WAYS)
        return pltpu.make_async_remote_copy(
            src_ref=part.at[way, c],
            dst_ref=got.at[way, c],
            send_sem=send_sem.at[way, c],
            recv_sem=recv_sem.at[way, c],
            device_id={"basis": to},
            device_id_type=MESH,
        )

    def serve(slot):
        for way in range(2):
            h = hops(way)
            c = slot - (h - 1)

            @pl.when((h >= 1) & (c >= 0) & (c < chunks))
            def _():
                copy = chunk_copy(way, c)
                copy.wait_recv()
                part[way, c] = part[way, c] + got[way, c]

                @pl.when(h < WAYS - 1)
                def _():
                    copy.start()

    def halves(basis):
        high = basis.astype(jnp.bfloat16)
        low = (basis - high.astype(jnp.float32)).astype(jnp.bfloat16)
        return high, low

    def product(rows_ref, way, first, size, basis, start, fresh):
        where = pl.ds(first, size)
        if basis is not None:
            high, low = halves(basis[...])
            split[where, pl.ds(0, EVECS)] = high
            split[where, pl.ds(EVECS, EVECS)] = low
        term = jnp.dot(
            rows_ref[pl.ds(way * half, half), where],
            split[where, :],
            preferred_element_type=jnp.float32,
        )
        if fresh:
            acc[...] = term
        else:
            acc[...] = acc[...] + term

    def give(way, base):
        value = acc[:, pl.ds(0, EVECS)] + acc[:, pl.ds(EVECS, EVECS)]
        part[way, pl.ds(base, per_block)] = value.reshape(per_block, ROWS, EVECS)

        @pl.when(hops(way) == 0)
        def _():
            for t in range(per_block):
                chunk_copy(way, base + t).start()

    loads[0].wait()
    for e in range(act_blocks):
        for way in range(2):
            if e == 0:
                loads[1 + way].wait()
            basis = act_basis.at[:, pl.ds(e * EVECS, EVECS)] if way == 0 else None
            product(act, way, 0, features, basis, 0, True)
            give(way, e * per_block)
    for i in range(1, grad_blocks):
        load_block(i).start()

    is_end = (z == 0) | (z == WAYS - 1)
    side = z // (WAYS - 1)

    def pair_copy():
        return pltpu.make_async_remote_copy(
            src_ref=squares.at[s],
            dst_ref=squares.at[s],
            send_sem=pair_sem.at[0],
            recv_sem=pair_sem.at[1],
            device_id={"sub": 1 - s},
            device_id_type=MESH,
        )

    def square_act():
        @pl.when(is_end)
        def _():
            for e in range(act_blocks):
                value = part[side, pl.ds(e * per_block, per_block)]
                squares[s, :, pl.ds(e * EVECS, EVECS)] = (value * value).reshape(half, EVECS)
            pair_copy().start()

    def x_copy(i):
        return pltpu.make_async_remote_copy(
            src_ref=x_out.at[i],
            dst_ref=x_in.at[i],
            send_sem=x_send.at[i],
            recv_sem=x_recv.at[i],
            device_id={"dp": 1 - d},
            device_id_type=MESH,
        )

    def final_copy(i, row, from_side):
        return pltpu.make_async_remote_copy(
            src_ref=sums.at[i],
            dst_ref=final.at[from_side],
            send_sem=final_send.at[i],
            recv_sem=final_recv.at[from_side],
            device_id={"basis": row},
            device_id_type=MESH,
        )

    def moments(i):
        value = part[side, pl.ds(act_chunks + i * per_block, per_block)]
        left = (value * value).reshape(half, EVECS).T

        def pairs(which):
            return jnp.dot(
                left,
                squares[which],
                precision=lax.Precision.HIGHEST,
                preferred_element_type=jnp.float32,
            )

        x_out[i] = pairs(1 - d)
        x_copy(i).start()
        sums[i] = pairs(d)

    def hand_over(i, row):
        x_copy(i).wait_recv()
        sums[i] = sums[i] + x_in[i]

        @pl.when(row != z)
        def _():
            final_copy(i, row, side).start()

    def block(b, carry):
        load_block_wait = pltpu.make_async_copy(
            grad_basis_hbm.at[:, pl.ds(0, EVECS)], grad_basis.at[b], load_sem.at[5 + b]
        )
        load_block_wait.wait()
        for way in range(2):

            @pl.when(b == 0)
            def _():
                loads[3 + way].wait()

            for step in range(STEPS):
                k = way * STEPS + step
                basis = grad_basis.at[b, pl.ds(step * piece, piece), :] if way == 0 else None
                product(grad, way, step * piece, piece, basis, 0, step == 0)
                if step == STEPS - 1:
                    give(way, act_chunks + b * per_block)
                if k % 2 == 1:
                    serve(jnp.where(b == 0, k, act_chunks + (b - 1) * per_block + k // 2))
                else:
                    pl.when(b == 0)(functools.partial(serve, k))
                if k == 3:
                    pl.when(b == 1)(square_act)

                    @pl.when((b >= 2) & is_end)
                    def _():
                        @pl.when(b == 2)
                        def _():
                            pair_copy().wait_recv()

                        moments(b - 2)

                if k == 7:

                    @pl.when((b >= 2) & is_end)
                    def _():
                        hand_over(b - 2, (b - 2) * (WAYS - 1))

        return carry

    lax.fori_loop(0, grad_blocks, block, 0)

    done = act_chunks + (grad_blocks - 1) * per_block
    for slot in range(done, done + 2):
        serve(slot)
    pl.when(is_end)(lambda: moments(2))
    for slot in range(done + 2, done + 6):
        serve(slot)

    @pl.when(is_end)
    def _():
        moments(3)
        hand_over(2, block_rows[2])
        hand_over(3, block_rows[3])

    @pl.when(z != 0)
    def _():
        final_copy(0, z, 0).wait_recv()

    @pl.when(z != WAYS - 1)
    def _():
        final_copy(0, z, 1).wait_recv()

    @pl.when(z == 0)
    def _():
        out_ref[...] = (sums[0] + final[1]) / total_tokens

    @pl.when(z == WAYS - 1)
    def _():
        out_ref[...] = (final[0] + sums[1]) / total_tokens

    @pl.when(jnp.logical_not(is_end))
    def _():
        out_ref[...] = (final[0] + final[1]) / total_tokens

    for way in range(2):

        @pl.when(hops(way) < WAYS - 1)
        def _():
            def drain(c, carry):
                chunk_copy(way, c).wait_send()
                return carry

            lax.fori_loop(0, chunks, drain, 0)

    @pl.when(is_end)
    def _():
        pair_copy().wait_send()
        for i in range(grad_blocks):
            x_copy(i).wait_send()

            @pl.when(z != block_rows[i])
            def _():
                final_copy(i, block_rows[i], side).wait_send()


def chained(activations, gradients, act_basis, grad_basis):
    tokens, act_features = activations.shape
    grad_features = gradients.shape[1]
    act_count, grad_count = act_basis.shape[1], grad_basis.shape[1]
    half = tokens // 2
    grad_blocks = grad_count // EVECS
    chunks = (act_count + grad_count) // EVECS * (half // ROWS)
    f32, bf16 = jnp.float32, jnp.bfloat16
    dma = pltpu.SemaphoreType.DMA
    return pl.pallas_call(
        functools.partial(chain_kernel, tokens * lax.axis_size("dp")),
        out_shape=jax.ShapeDtypeStruct((EVECS, act_count), f32),
        in_specs=[pl.BlockSpec(memory_space=pl.ANY)] * 4,
        out_specs=pl.BlockSpec(memory_space=pltpu.VMEM),
        scratch_shapes=[
            pltpu.VMEM((tokens, act_features), bf16),
            pltpu.VMEM((tokens, grad_features), bf16),
            pltpu.VMEM((act_features, act_count), f32),
            pltpu.VMEM((grad_blocks, grad_features, EVECS), f32),
            pltpu.VMEM((max(grad_features, act_features), 2 * EVECS), bf16),
            pltpu.VMEM((half, 2 * EVECS), f32),
            pltpu.VMEM((2, chunks, ROWS, EVECS), f32),
            pltpu.VMEM((2, chunks, ROWS, EVECS), f32),
            pltpu.VMEM((2, half, act_count), f32),
            pltpu.VMEM((grad_blocks, EVECS, act_count), f32),
            pltpu.VMEM((grad_blocks, EVECS, act_count), f32),
            pltpu.VMEM((grad_blocks, EVECS, act_count), f32),
            pltpu.VMEM((2, EVECS, act_count), f32),
            dma((5 + grad_blocks,)),
            dma((2, chunks)),
            dma((2, chunks)),
            dma((2,)),
            dma((grad_blocks,)),
            dma((grad_blocks,)),
            dma((grad_blocks,)),
            dma((2,)),
        ],
        compiler_params=pltpu.CompilerParams(
            collective_id=0, has_side_effects=True, vmem_limit_bytes=60 * 1024 * 1024
        ),
    )(activations, gradients, act_basis, grad_basis)


def split_basis(basis):
    high = lax.reduce_precision(basis, 8, 7)
    return high.astype(jnp.bfloat16), (basis - high).astype(jnp.bfloat16)


def make_term(basis, rows_in):
    dims = (((0,), (1,)), ((), ()))
    high, low = split_basis(basis)
    return lax.dot_general(
        high, rows_in, dims, preferred_element_type=jnp.float32
    ) + lax.dot_general(low, rows_in, dims, preferred_element_type=jnp.float32)


def pair_products(left, right):
    return lax.dot_general(
        left,
        right,
        (((1,), (1,)), ((), ())),
        precision=lax.Precision.HIGHEST,
        preferred_element_type=jnp.float32,
    )


def body(activations, gradients, act_basis, grad_basis):
    full_act = lax.psum(make_term(act_basis, activations), "basis")
    own_grad = lax.psum_scatter(
        make_term(grad_basis, gradients), "basis", scatter_dimension=0, tiled=True
    )
    squared_act = lax.all_gather(full_act * full_act, "sub", axis=0, tiled=True)
    partial_sums = pair_products(own_grad * own_grad, squared_act)
    summed = lax.psum_scatter(partial_sums, "dp", scatter_dimension=1, tiled=True)
    return summed / (activations.shape[0] * lax.axis_size("dp"))


def solution(mesh):
    sizes = mesh.shape
    fits = sizes["basis"] == WAYS and sizes["dp"] == 2 and sizes["sub"] == 2

    def per_device(activations, gradients, act_basis, grad_basis):
        even = activations.shape[0] % (2 * ROWS) == 0
        blocks = act_basis.shape[1] % EVECS == 0 and grad_basis.shape[1] == WAYS * EVECS
        if fits and even and blocks:
            return chained(activations, gradients, act_basis, grad_basis)
        return body(activations, gradients, act_basis, grad_basis)

    return jax.shard_map(
        per_device,
        mesh=mesh,
        in_specs=(
            P(("groups", "dp"), "basis"),
            P(("groups", "dp"), "basis"),
            P(("groups", "basis"), "sub"),
            P(("groups", "basis"), "sub"),
        ),
        out_specs=P(("groups", "sub", "basis"), "dp"),
        check_vma=False,
    )
```

```python
import functools

import jax
import jax.numpy as jnp
from jax import lax
from jax.experimental import pallas as pl
from jax.experimental.pallas import tpu as pltpu
from jax.sharding import PartitionSpec as P

MESH = pl.DeviceIdType.MESH
WAYS = 4
EVECS = 128
ROWS = 128
STEPS = 4
LAG = 2


def chain_kernel(
    total_tokens,
    act_hbm,
    grad_hbm,
    act_basis_hbm,
    grad_basis_hbm,
    out_ref,
    act,
    grad,
    act_basis,
    grad_basis,
    split,
    acc,
    part,
    got,
    squares,
    x_out,
    x_in,
    sums,
    final,
    load_sem,
    send_sem,
    recv_sem,
    pair_sem,
    x_send,
    x_recv,
    final_send,
    final_recv,
):
    z = lax.axis_index("basis")
    d = lax.axis_index("dp")
    s = lax.axis_index("sub")
    tokens, features = act.shape
    half = tokens // 2
    act_blocks = act_basis.shape[1] // EVECS
    grad_blocks = grad_basis.shape[0]
    per_block = half // ROWS
    chunks = part.shape[1]
    act_chunks = act_blocks * per_block
    piece = grad.shape[1] // STEPS
    block_rows = (0, 3, 1, 2)

    barrier = pltpu.get_barrier_semaphore()
    for hop in range(1, WAYS):
        pl.semaphore_signal(
            barrier, inc=1, device_id={"basis": lax.rem(z + hop, WAYS)}, device_id_type=MESH
        )
    pl.semaphore_signal(barrier, inc=1, device_id={"dp": 1 - d}, device_id_type=MESH)
    pl.semaphore_signal(barrier, inc=1, device_id={"sub": 1 - s}, device_id_type=MESH)

    loads = [pltpu.make_async_copy(act_basis_hbm, act_basis, load_sem.at[0])]
    for way in range(2):
        rows = pl.ds(way * half, half)
        loads.append(
            pltpu.make_async_copy(act_hbm.at[rows, :], act.at[rows, :], load_sem.at[1 + way])
        )
    for way in range(2):
        rows = pl.ds(way * half, half)
        loads.append(
            pltpu.make_async_copy(grad_hbm.at[rows, :], grad.at[rows, :], load_sem.at[3 + way])
        )

    def load_block(i):
        column = block_rows[i] * EVECS
        return pltpu.make_async_copy(
            grad_basis_hbm.at[:, pl.ds(column, EVECS)], grad_basis.at[i], load_sem.at[5 + i]
        )

    for load in loads[:3]:
        load.start()
    load_block(0).start()
    for load in loads[3:]:
        load.start()
    pl.semaphore_wait(barrier, WAYS + 1)

    def hops(way):
        return z if way else WAYS - 1 - z

    def chunk_copy(way, c):
        to = lax.rem(z + (1 if way else WAYS - 1), WAYS)
        return pltpu.make_async_remote_copy(
            src_ref=part.at[way, c],
            dst_ref=got.at[way, c],
            send_sem=send_sem.at[way, c],
            recv_sem=recv_sem.at[way, c],
            device_id={"basis": to},
            device_id_type=MESH,
        )

    def serve(slot):
        for way in range(2):
            h = hops(way)
            c = slot - LAG * (h - 1)

            @pl.when((h >= 1) & (c >= 0) & (c < chunks))
            def _():
                copy = chunk_copy(way, c)
                copy.wait_recv()
                part[way, c] = part[way, c] + got[way, c]

                @pl.when(h < WAYS - 1)
                def _():
                    copy.start()

    def halves(basis):
        high = basis.astype(jnp.bfloat16)
        low = (basis - high.astype(jnp.float32)).astype(jnp.bfloat16)
        return high, low

    def product(rows_ref, way, first, size, basis, start, fresh):
        where = pl.ds(first, size)
        if basis is not None:
            high, low = halves(basis[...])
            split[where, pl.ds(0, EVECS)] = high
            split[where, pl.ds(EVECS, EVECS)] = low
        term = jnp.dot(
            rows_ref[pl.ds(way * half, half), where],
            split[where, :],
            preferred_element_type=jnp.float32,
        )
        if fresh:
            acc[...] = term
        else:
            acc[...] = acc[...] + term

    def give(way, base):
        value = acc[:, pl.ds(0, EVECS)] + acc[:, pl.ds(EVECS, EVECS)]
        part[way, pl.ds(base, per_block)] = value.reshape(per_block, ROWS, EVECS)

        @pl.when(hops(way) == 0)
        def _():
            for t in range(per_block):
                chunk_copy(way, base + t).start()

    loads[0].wait()
    for e in range(act_blocks):
        for way in range(2):
            if e == 0:
                loads[1 + way].wait()
            basis = act_basis.at[:, pl.ds(e * EVECS, EVECS)] if way == 0 else None
            product(act, way, 0, features, basis, 0, True)
            give(way, e * per_block)
    for i in range(1, grad_blocks):
        load_block(i).start()

    is_end = (z == 0) | (z == WAYS - 1)
    side = z // (WAYS - 1)

    def pair_copy():
        return pltpu.make_async_remote_copy(
            src_ref=squares.at[s],
            dst_ref=squares.at[s],
            send_sem=pair_sem.at[0],
            recv_sem=pair_sem.at[1],
            device_id={"sub": 1 - s},
            device_id_type=MESH,
        )

    def square_act():
        @pl.when(is_end)
        def _():
            for e in range(act_blocks):
                value = part[side, pl.ds(e * per_block, per_block)]
                squares[s, :, pl.ds(e * EVECS, EVECS)] = (value * value).reshape(half, EVECS)
            pair_copy().start()

    def x_copy(i):
        return pltpu.make_async_remote_copy(
            src_ref=x_out.at[i],
            dst_ref=x_in.at[i],
            send_sem=x_send.at[i],
            recv_sem=x_recv.at[i],
            device_id={"dp": 1 - d},
            device_id_type=MESH,
        )

    def final_copy(i, row, from_side):
        return pltpu.make_async_remote_copy(
            src_ref=sums.at[i],
            dst_ref=final.at[from_side],
            send_sem=final_send.at[i],
            recv_sem=final_recv.at[from_side],
            device_id={"basis": row},
            device_id_type=MESH,
        )

    def moments(i):
        value = part[side, pl.ds(act_chunks + i * per_block, per_block)]
        left = (value * value).reshape(half, EVECS).T

        left_high, left_low = halves(left)

        def pairs(which):
            high, low = halves(squares[which])
            return (
                jnp.dot(left_high, high, preferred_element_type=jnp.float32)
                + jnp.dot(left_high, low, preferred_element_type=jnp.float32)
                + jnp.dot(left_low, high, preferred_element_type=jnp.float32)
            )

        x_out[i] = pairs(1 - d)
        x_copy(i).start()
        sums[i] = pairs(d)

    def hand_over(i, row):
        x_copy(i).wait_recv()
        sums[i] = sums[i] + x_in[i]

        @pl.when(row != z)
        def _():
            final_copy(i, row, side).start()

    def block(b, carry):
        load_block_wait = pltpu.make_async_copy(
            grad_basis_hbm.at[:, pl.ds(0, EVECS)], grad_basis.at[b], load_sem.at[5 + b]
        )
        load_block_wait.wait()
        for way in range(2):

            @pl.when(b == 0)
            def _():
                loads[3 + way].wait()

            for step in range(STEPS):
                k = way * STEPS + step
                basis = grad_basis.at[b, pl.ds(step * piece, piece), :] if way == 0 else None
                product(grad, way, step * piece, piece, basis, 0, step == 0)
                if step == STEPS - 1:
                    give(way, act_chunks + b * per_block)
                if k % 2 == 1:
                    serve(jnp.where(b == 0, k, act_chunks + (b - 1) * per_block + k // 2))
                else:
                    pl.when(b == 0)(functools.partial(serve, k))
                if k == 7:
                    pl.when(b == 1)(square_act)

                    @pl.when((b == 2) & is_end)
                    def _():
                        pair_copy().wait_recv()
                        moments(0)

                    @pl.when((b == 3) & is_end)
                    def _():
                        hand_over(0, block_rows[0])
                        moments(1)

        return carry

    lax.fori_loop(0, grad_blocks, block, 0)

    done = act_chunks + (grad_blocks - 1) * per_block
    for slot in range(done, done + LAG):
        serve(slot)
    pl.when(is_end)(lambda: hand_over(1, block_rows[1]))
    for slot in range(done + LAG, done + 2 * LAG):
        serve(slot)
    pl.when(is_end)(lambda: moments(2))
    for slot in range(done + 2 * LAG, chunks + 2 * LAG):
        serve(slot)

    @pl.when(is_end)
    def _():
        moments(3)
        hand_over(2, block_rows[2])
        hand_over(3, block_rows[3])

    @pl.when(z != 0)
    def _():
        final_copy(0, z, 0).wait_recv()

    @pl.when(z != WAYS - 1)
    def _():
        final_copy(0, z, 1).wait_recv()

    @pl.when(z == 0)
    def _():
        out_ref[...] = (sums[0] + final[1]) / total_tokens

    @pl.when(z == WAYS - 1)
    def _():
        out_ref[...] = (final[0] + sums[1]) / total_tokens

    @pl.when(jnp.logical_not(is_end))
    def _():
        out_ref[...] = (final[0] + final[1]) / total_tokens

    for way in range(2):

        @pl.when(hops(way) < WAYS - 1)
        def _():
            def drain(c, carry):
                chunk_copy(way, c).wait_send()
                return carry

            lax.fori_loop(0, chunks, drain, 0)

    @pl.when(is_end)
    def _():
        pair_copy().wait_send()
        for i in range(grad_blocks):
            x_copy(i).wait_send()

            @pl.when(z != block_rows[i])
            def _():
                final_copy(i, block_rows[i], side).wait_send()


def chained(activations, gradients, act_basis, grad_basis):
    tokens, act_features = activations.shape
    grad_features = gradients.shape[1]
    act_count, grad_count = act_basis.shape[1], grad_basis.shape[1]
    half = tokens // 2
    grad_blocks = grad_count // EVECS
    chunks = (act_count + grad_count) // EVECS * (half // ROWS)
    f32, bf16 = jnp.float32, jnp.bfloat16
    dma = pltpu.SemaphoreType.DMA
    return pl.pallas_call(
        functools.partial(chain_kernel, tokens * lax.axis_size("dp")),
        out_shape=jax.ShapeDtypeStruct((EVECS, act_count), f32),
        in_specs=[pl.BlockSpec(memory_space=pl.ANY)] * 4,
        out_specs=pl.BlockSpec(memory_space=pltpu.VMEM),
        scratch_shapes=[
            pltpu.VMEM((tokens, act_features), bf16),
            pltpu.VMEM((tokens, grad_features), bf16),
            pltpu.VMEM((act_features, act_count), f32),
            pltpu.VMEM((grad_blocks, grad_features, EVECS), f32),
            pltpu.VMEM((max(grad_features, act_features), 2 * EVECS), bf16),
            pltpu.VMEM((half, 2 * EVECS), f32),
            pltpu.VMEM((2, chunks, ROWS, EVECS), f32),
            pltpu.VMEM((2, chunks, ROWS, EVECS), f32),
            pltpu.VMEM((2, half, act_count), f32),
            pltpu.VMEM((grad_blocks, EVECS, act_count), f32),
            pltpu.VMEM((grad_blocks, EVECS, act_count), f32),
            pltpu.VMEM((grad_blocks, EVECS, act_count), f32),
            pltpu.VMEM((2, EVECS, act_count), f32),
            dma((5 + grad_blocks,)),
            dma((2, chunks)),
            dma((2, chunks)),
            dma((2,)),
            dma((grad_blocks,)),
            dma((grad_blocks,)),
            dma((grad_blocks,)),
            dma((2,)),
        ],
        compiler_params=pltpu.CompilerParams(
            collective_id=0, has_side_effects=True, vmem_limit_bytes=60 * 1024 * 1024
        ),
    )(activations, gradients, act_basis, grad_basis)


def split_basis(basis):
    high = lax.reduce_precision(basis, 8, 7)
    return high.astype(jnp.bfloat16), (basis - high).astype(jnp.bfloat16)


def make_term(basis, rows_in):
    dims = (((0,), (1,)), ((), ()))
    high, low = split_basis(basis)
    return lax.dot_general(
        high, rows_in, dims, preferred_element_type=jnp.float32
    ) + lax.dot_general(low, rows_in, dims, preferred_element_type=jnp.float32)


def pair_products(left, right):
    return lax.dot_general(
        left,
        right,
        (((1,), (1,)), ((), ())),
        precision=lax.Precision.HIGHEST,
        preferred_element_type=jnp.float32,
    )


def body(activations, gradients, act_basis, grad_basis):
    full_act = lax.psum(make_term(act_basis, activations), "basis")
    own_grad = lax.psum_scatter(
        make_term(grad_basis, gradients), "basis", scatter_dimension=0, tiled=True
    )
    squared_act = lax.all_gather(full_act * full_act, "sub", axis=0, tiled=True)
    partial_sums = pair_products(own_grad * own_grad, squared_act)
    summed = lax.psum_scatter(partial_sums, "dp", scatter_dimension=1, tiled=True)
    return summed / (activations.shape[0] * lax.axis_size("dp"))


def solution(mesh):
    sizes = mesh.shape
    fits = sizes["basis"] == WAYS and sizes["dp"] == 2 and sizes["sub"] == 2

    def per_device(activations, gradients, act_basis, grad_basis):
        even = activations.shape[0] % (2 * ROWS) == 0
        blocks = act_basis.shape[1] % EVECS == 0 and grad_basis.shape[1] == WAYS * EVECS
        if fits and even and blocks:
            return chained(activations, gradients, act_basis, grad_basis)
        return body(activations, gradients, act_basis, grad_basis)

    return jax.shard_map(
        per_device,
        mesh=mesh,
        in_specs=(
            P(("groups", "dp"), "basis"),
            P(("groups", "dp"), "basis"),
            P(("groups", "basis"), "sub"),
            P(("groups", "basis"), "sub"),
        ),
        out_specs=P(("groups", "sub", "basis"), "dp"),
        check_vma=False,
    )
```
